32 devices in a mesh: group: 2 (over y), outer: 4 (over z), blk: 2 (over x), hid: 2 (over core).
Axes of the slice: x: 2, y: 2, z: 4, core: 2. Of those that a mesh axis runs over, the one named last changes fastest.
Arguments:
- tokens: bfloat16 [2048, 3584], P(('group', 'outer', 'blk')), parts along dimension 0, may hold values from -6 to 6
- routes: int32 [2048, 2], P(('group', 'outer', 'blk')), parts along dimension 0, may hold values from 0 to 3, all different within a row; in each aligned block of 128 rows (0 to 127, 128 to 255, ...) at most 80 rows name the same one
- scores: float32 [2048, 2], P(('group', 'outer', 'blk')), parts along dimension 0, may hold values from 0.1 to 1
- gate_weight: bfloat16 [4, 2048, 3584], P('outer', ('blk', 'hid')), may hold values from -0.09375 to 0.09375
- up_weight: bfloat16 [4, 2048, 3584], P('outer', ('blk', 'hid')), may hold values from -0.09375 to 0.09375
- down_weight: bfloat16 [4, 2048, 3584], P('outer', ('blk', 'hid')), may hold values from -0.125 to 0.125
Outputs:
- mixed: bfloat16 [2048, 3584], P(('group', 'outer', 'blk'), 'hid'), parts along dimension 0
The draws below stay inside these ranges and needn't reach their ends.
There are 2 independent parts, one for each index of `group`. The reference program is written for one: setup_inputs(seed, part) draws one part's arguments, and reference() takes and returns one part's arrays. A program takes and returns all parts, laid end to end along the dimension named above; an argument that names none is the same for every part. Nothing has to cross between parts.
Inputs may be any that keep to these rules, and one draw needn't show every extreme that they name: `routes`: each token names 2 different experts. In the rows of one device (aligned blocks of 128 tokens) no expert is named more than 80 times, and in some blocks of every draw some expert is named exactly 80 times.
All inputs are finite; a program needn't handle non-finite values.
Results may differ from the reference program's by a relative error of at most 0.0067.
Values may be sent and summed in bfloat16 or wider, within the bound.
A program may use at most 128 MiB of HBM per device.

```python
import math
import jax
import jax.numpy as jnp
import numpy as np
from jax import lax

D = 3584
FF = 2048
TOPK = 2
TOK_DEV = 128
EXPERTS = 4
TOKENS = 1024
CAP = 80
N_BLK = 2
N_HID = 2


def block_scale(key, extent, split, low, top_value):
    def one(dim, shards_of):
        steps = jax.random.uniform(jax.random.fold_in(jax.random.fold_in(key, 6), dim), (shards_of,), jnp.float32, low / len(split), top_value / len(split))
        return jnp.repeat(jnp.exp(steps), extent[dim] // shards_of).reshape((-1,) + (1,) * (len(extent) - dim - 1))

    gain = one(*split[0])
    for cut in split[1:]:
        gain = gain * one(*cut)
    return gain


def deal_out(key, own, number, rows, count, top, limit, slope):
    sequence = jax.random.permutation(key, count)
    heavy_load, common = portions_of(count, rows * top, limit, slope, True), portions_of(count, rows * top, limit, slope, False)
    places = jnp.arange(count)

    def named(lengths, rotation):
        used = int((lengths > 0).sum())
        fixed = max(1, used // 4)
        moved = fixed + (places - fixed + rotation * (used - fixed)) % max(1, count - fixed)
        return jnp.zeros((count,), jnp.int32).at[sequence[jnp.where(places < fixed, places, moved)]].set(jnp.asarray(lengths, jnp.int32))

    lengths = jnp.where(number % 4 == 0, named(heavy_load, number // 4), named(common, number - number // 4 - 1))
    mixed = jax.random.permutation(jax.random.fold_in(own, 3), count)
    giver, receiver = mixed[0:count // 2 * 2:2], mixed[1:count // 2 * 2:2]
    room = jnp.minimum(lengths[giver] - 1, limit - lengths[receiver]) // 2
    room = jnp.where((giver == sequence[0]) | (receiver == sequence[0]) | (lengths[receiver] == 0), 0, jnp.maximum(room, 0))
    moved = jax.random.randint(jax.random.fold_in(own, 4), (count // 2,), 0, 1 << 20) % (room + 1)
    lengths = lengths.at[giver].add(-moved).at[receiver].add(moved)
    items = jnp.searchsorted(jnp.cumsum(lengths), jnp.arange(rows * top), side="right").astype(jnp.int32)
    grid = items.reshape(top, rows).T
    grid = grid[jax.random.permutation(jax.random.fold_in(own, 1), rows)]
    rotation = jax.random.randint(jax.random.fold_in(own, 2), (rows, 1), 0, top)
    return jnp.take_along_axis(grid, (jnp.arange(top)[None, :] + rotation) % top, axis=1)


def portions_of(number_of, total, bound, lean, full):
    portions = [(1 << 20) // math.isqrt(grade ** lean) + 1 for grade in range(1, number_of + 1)]
    largest = bound if full else min(bound, max(-(-total // number_of), total * portions[0] // sum(portions)))
    least = 1 if total - largest >= number_of - 1 else 0
    given, surplus = [largest] + [least] * (number_of - 1), total - largest - least * (number_of - 1)
    while surplus > 0:
        movable = [i for i in range(1, number_of) if given[i] < largest] or [i for i in range(1, number_of) if given[i] < bound]
        pool, remaining = sum([portions[i] for i in movable]), surplus
        for i in movable:
            extra = min(bound - given[i], max(1, remaining * portions[i] // pool), surplus)
            given[i] = given[i] + extra
            surplus = surplus - extra
    return np.array(given)


def scatter_about(rng, dims, spread, most, cuts=(), held_as=jnp.bfloat16):
    values = spread * jax.random.normal(rng, dims, jnp.float32)
    if cuts:
        values = values * block_scale(rng, dims, cuts, -0.22, 0.18)
    return jnp.clip(values, -most, most).astype(held_as)


def setup_inputs(seed: int = 0, part: int = 0) -> dict:
    arg_keys = jax.random.split(jax.random.key(seed), 7)
    own_keys = jax.random.split(jax.random.fold_in(arg_keys[6], part), 7)
    tokens = scatter_about(own_keys[0], (TOKENS, D), 1.0, 6.0, ((0, 8),))
    routes_keys = jax.random.split(jax.random.fold_in(own_keys[1], 1), TOKENS // TOK_DEV)
    routes_turns = jax.random.permutation(jax.random.fold_in(own_keys[1], 3), TOKENS // TOK_DEV)
    routes = jax.vmap(lambda own, number: deal_out(jax.random.fold_in(own_keys[1], 2), own, number, TOK_DEV, EXPERTS, TOPK, CAP, 2))(routes_keys, routes_turns).reshape((TOKENS, TOPK))
    scores = jnp.clip(jnp.exp(math.log(1.0) - 2.3025851 * jax.random.uniform(own_keys[2], (TOKENS, TOPK), jnp.float32) ** block_scale(own_keys[2], (TOKENS, TOPK), ((0, 8),), -0.2, 0.2)), 0.1, 1.0)
    gate_weight = scatter_about(arg_keys[3], (EXPERTS, FF, D), D ** -0.5, 0.09375, ((0, 4), (1, 4)))
    up_weight = scatter_about(arg_keys[4], (EXPERTS, FF, D), D ** -0.5, 0.09375, ((0, 4), (1, 4)))
    down_weight = scatter_about(arg_keys[5], (EXPERTS, FF, D), FF ** -0.5, 0.125, ((0, 4), (1, 4)))
    return {"tokens": tokens, "routes": routes, "scores": scores, "gate_weight": gate_weight, "up_weight": up_weight, "down_weight": down_weight}


route_scale = 2.5


def reference(tokens, routes, scores, gate_weight, up_weight, down_weight):
    blocks = TOKENS // TOK_DEV
    per_block = TOK_DEV * TOPK
    flat = routes.reshape(blocks, per_block).astype(jnp.int32)
    onehot = (flat[:, :, None] == jnp.arange(EXPERTS, dtype=jnp.int32)[None, None, :]).astype(jnp.int32)
    rank = jnp.sum((jnp.cumsum(onehot, axis=1) - onehot) * onehot, axis=2)
    places = flat * (blocks * CAP) + jnp.arange(blocks, dtype=jnp.int32)[:, None] * CAP + rank
    empty_route = TOKENS * TOPK
    table = jnp.full((EXPERTS * blocks * CAP,), empty_route, jnp.int32)
    table = table.at[places.reshape(-1)].set(jnp.arange(TOKENS * TOPK, dtype=jnp.int32))
    table = table.reshape(EXPERTS, blocks * CAP)
    weights = route_scale * scores / jnp.sum(scores, axis=1, keepdims=True)
    weight_list = jnp.concatenate([weights.reshape(-1), jnp.zeros((1,), jnp.float32)])
    padded = jnp.concatenate([tokens, jnp.zeros((1, D), tokens.dtype)])
    slice_units = FF // (N_BLK * N_HID)

    def one_expert(total, expert):
        chosen = table[expert]
        owners = chosen // TOPK
        rows = padded[owners].astype(jnp.float32)
        gate_part = jnp.dot(rows, gate_weight[expert].astype(jnp.float32).T, precision=lax.Precision.HIGHEST)
        up_part = jnp.dot(rows, up_weight[expert].astype(jnp.float32).T, precision=lax.Precision.HIGHEST)
        hidden = lax.optimization_barrier((jax.nn.silu(gate_part) * up_part).astype(jnp.bfloat16)).astype(jnp.float32)
        split_hidden = hidden.reshape(-1, N_BLK, N_HID, slice_units)
        split_down = down_weight[expert].astype(jnp.float32).reshape(N_BLK, N_HID, slice_units, D)
        partial_value = jnp.einsum("rbhj,bhjd->rhd", split_hidden, split_down, precision=lax.Precision.HIGHEST)
        partial_value = lax.optimization_barrier(partial_value.astype(jnp.bfloat16)).astype(jnp.float32)
        expert_out = lax.optimization_barrier(jnp.sum(partial_value, axis=1).astype(jnp.bfloat16)).astype(jnp.float32)
        total = total.at[owners].add(weight_list[chosen][:, None] * expert_out)
        return total, None

    total, unused = lax.scan(one_expert, jnp.zeros((TOKENS + 1, D), jnp.float32), jnp.arange(EXPERTS, dtype=jnp.int32))
    return total[:TOKENS].astype(jnp.bfloat16)
```

```python
import functools
import jax
import jax.numpy as jnp
from jax import lax
from jax.experimental import pallas as pl
from jax.experimental.pallas import tpu as pltpu
from jax.sharding import PartitionSpec as P

route_scale = 2.5
PIECES = 7
WINDOW = 2
ROUND_PARTS = (1,)
SEND_ORDER = (2, 3, 1)


def slice_terms(rows, gate_piece, up_piece, down_piece):
    dims = (((1,), (1,)), ((), ()))
    gate_part = lax.dot_general(rows, gate_piece, dims, preferred_element_type=jnp.float32)
    up_part = lax.dot_general(rows, up_piece, dims, preferred_element_type=jnp.float32)
    hidden = (jax.nn.silu(gate_part) * up_part).astype(jnp.bfloat16)
    return jnp.dot(hidden, down_piece, preferred_element_type=jnp.float32)


def local(tokens, routes, scores, gate_weight, up_weight, down_weight):
    tok_dev, width = tokens.shape
    topk = routes.shape[1]
    experts = lax.axis_size("outer")
    shares = lax.axis_size("hid")
    half = width // shares
    capacity = (tok_dev * topk * 5 // experts + 3) // 4
    flat = routes.reshape(-1)
    onehot = (flat[:, None] == jnp.arange(experts, dtype=jnp.int32)[None, :]).astype(jnp.int32)
    before = jnp.cumsum(onehot, axis=0) - onehot
    rank = jnp.sum(before * onehot, axis=1)
    slots = flat * capacity + rank
    owner = jnp.arange(tok_dev * topk, dtype=jnp.int32) // topk
    columns = tokens.shape[1]
    send = jnp.zeros((experts * capacity, columns), jnp.bfloat16).at[slots].set(tokens[owner])
    send = send.reshape(experts, capacity, columns)
    gate_local = gate_weight[0]
    up_local = up_weight[0]
    down_local = down_weight[0]
    arrived = lax.all_to_all(send, "outer", split_axis=0, concat_axis=0, tiled=True)
    senders, count, unused = arrived.shape
    rows = arrived.reshape(senders * count, width)
    total = slice_terms(
        rows,
        lax.all_gather(gate_local, "blk", axis=0, tiled=True),
        lax.all_gather(up_local, "blk", axis=0, tiled=True),
        lax.all_gather(down_local, "blk", axis=0, tiled=True),
    )
    summed = lax.psum(total.astype(jnp.bfloat16), "hid").astype(jnp.float32)
    share = lax.dynamic_slice_in_dim(summed, lax.axis_index("hid") * half, half, 1)
    answered = share.astype(jnp.bfloat16).reshape(senders, count, half)
    returned = lax.all_to_all(answered, "outer", split_axis=0, concat_axis=0, tiled=True)
    picked = (
        returned.reshape(experts * capacity, half)[slots]
        .astype(jnp.float32)
        .reshape(tok_dev, topk, half)
    )
    weights = route_scale * scores / jnp.sum(scores, axis=1, keepdims=True)
    mixed = jnp.sum(weights[:, :, None] * picked, axis=1)
    return mixed.astype(jnp.bfloat16)


MESH = pl.DeviceIdType.MESH
bf16, f32 = jnp.bfloat16, jnp.float32


def partner(z, d):
    if d == 1:
        return z + 1 - 2 * lax.rem(z, 2)
    if d == 2:
        return lax.rem(z + 2, 4)
    if d == 3:
        return 3 - z
    return z


def layer_kernel(rounds, pieces, tok, routes, scores, gate_hbm, up_hbm, down_hbm, out,
                 tokv, gw, uw, dw, buffers, local_sem, z_s, z_r, sem_s, sem_r, back_s, back_r):
    z, x, h = lax.axis_index("outer"), lax.axis_index("blk"), lax.axis_index("hid")
    steps = buffers[0]["send"].shape[1]
    half, units = tokv.shape[1], gw.shape[0]
    piece = half // pieces
    ox, oh = 1 - x, 1 - h
    col0 = pl.multiple_of(h * half, 128)

    load_tok = pltpu.make_async_copy(tok.at[:, pl.ds(col0, half)], tokv, local_sem.at[0])
    load_tok.start()
    loads = [
        pltpu.make_async_copy(src.at[0], dst, local_sem.at[1 + i])
        for i, (src, dst) in enumerate(((gate_hbm, gw), (up_hbm, uw), (down_hbm, dw)))
    ]

    barrier = pltpu.get_barrier_semaphore()
    peers = [{"outer": partner(z, d)} for d in range(1, steps)] + [{"blk": ox}, {"hid": oh}]
    for peer in peers:
        pl.semaphore_signal(barrier, inc=1, device_id=peer, device_id_type=MESH)

    tokens = routes.shape[0]
    below = lax.broadcasted_iota(jnp.int32, (tokens, tokens), 1) < lax.broadcasted_iota(
        jnp.int32, (tokens, tokens), 0)
    below = jnp.where(below, 1.0, 0.0).astype(bf16)
    weight = route_scale * scores[...] / (scores[:, 0:1] + scores[:, 1:2])
    places, mixes = [], []
    start = 0
    for c in rounds:
        wide = (tokens, steps * c)
        lane = lax.broadcasted_iota(jnp.int32, wide, 1)
        expert = lane // c
        first = routes[:, 0:1] == expert
        second = routes[:, 1:2] == expert
        named = jnp.where(first | second, 1.0, 0.0)
        rank = jnp.dot(below, named.astype(bf16), preferred_element_type=f32)
        slot = (lane - expert * c + start).astype(f32)
        place = jnp.where(rank == slot, named, 0.0)
        mix = place * (jnp.where(first, weight[:, 0:1], 0.0) + jnp.where(second, weight[:, 1:2], 0.0))
        mix_high = mix.astype(bf16)
        places.append(place.astype(bf16))
        mixes.append((mix_high, (mix - mix_high.astype(f32)).astype(bf16)))
        start += c

    where = [partner(z, d) for d in range(steps)]

    def remote(src, dst, send_sem, recv_sem, peer):
        return pltpu.make_async_remote_copy(
            src_ref=src, dst_ref=dst, send_sem=send_sem, recv_sem=recv_sem,
            device_id=peer, device_id_type=MESH)

    work = [(r, p) for r in range(len(rounds)) for p in range(pieces)]
    to_expert, across, beside, beside2, sum_hid, sum_blk, back = {}, {}, {}, {}, {}, {}, {}
    for n, (r, p) in enumerate(work):
        bufs, key = buffers[r], (r, p)
        rows = bufs["rows"]
        to_expert[key] = [
            remote(bufs["send"].at[p, where[d]], rows.at[p, h, x, z], z_s.at[n, d], z_r.at[n, d], {"outer": where[d]})
            for d in SEND_ORDER]
        across[key] = remote(rows.at[p, h, x], rows.at[p, h, x], sem_s.at[0, n], sem_r.at[0, n], {"blk": ox})
        beside[key] = remote(rows.at[p, h, x], rows.at[p, h, x], sem_s.at[1, n], sem_r.at[1, n], {"hid": oh})
        beside2[key] = remote(rows.at[p, h, ox], rows.at[p, h, ox], sem_s.at[2, n], sem_r.at[2, n], {"hid": oh})
        sum_hid[key] = remote(bufs["a_send"].at[p], bufs["a_recv"].at[p], sem_s.at[3, n], sem_r.at[3, n], {"hid": oh})
        sum_blk[key] = remote(bufs["b_send"].at[p], bufs["b_recv"].at[p], sem_s.at[4, n], sem_r.at[4, n], {"blk": ox})
        back[key] = [
            remote(bufs["c_send"].at[p, where[d]], bufs["ret"].at[p, z], back_s.at[n, d], back_r.at[n, d], {"outer": where[d]})
            for d in SEND_ORDER]

    load_tok.wait()

    def build(r, p):
        sent = lax.dot_general(
            places[r], tokv[:, p * piece:(p + 1) * piece], (((0,), (0,)), ((), ())), preferred_element_type=f32)
        buffers[r]["send"][p] = sent.astype(bf16).reshape(steps, rounds[r], piece)
        if (r, p) == work[0]:
            pl.semaphore_wait(barrier, len(peers))
        if work.index((r, p)) < WINDOW:
            for copy in to_expert[r, p]:
                copy.start()
        buffers[r]["rows"][p, h, x, z] = buffers[r]["send"][p, z]

    def forward(r, p):
        n = work.index((r, p)) + WINDOW
        if n < len(work):
            for copy in to_expert[work[n]]:
                copy.start()
        for copy in to_expert[r, p]:
            copy.wait_recv()
        across[r, p].start()
        beside[r, p].start()

    def forward2(r, p):
        across[r, p].wait_recv()
        beside2[r, p].start()

    nt = (((1,), (1,)), ((), ()))

    def compute(r, p):
        bufs = buffers[r]
        rows, gate, up = bufs["rows"], bufs["gate"], bufs["up"]
        beside[r, p].wait_recv()
        beside2[r, p].wait_recv()
        if (r, p) == work[0]:
            loads[0].wait()
            loads[1].wait()
        parts = [rows[p, k].reshape(gate.shape[0], piece) for k in range(2)]

        @pl.loop(0, units // 256)
        def _(j):
            take = pl.ds(pl.multiple_of(j * 256, 256), 256)
            for total, weights in ((gate, gw), (up, uw)):
                value = sum(
                    lax.dot_general(
                        parts[k], weights[take, k * half + p * piece:k * half + (p + 1) * piece], nt,
                        preferred_element_type=f32)
                    for k in range(2))
                total[:, take] = value if p == 0 else total[:, take] + value

    def activate(r, p):
        bufs = buffers[r]
        gate, up, hidden = bufs["gate"], bufs["up"], bufs["hidden"]

        @pl.loop(0, gate.shape[0] // 32)
        def _(j):
            take = pl.ds(pl.multiple_of(j * 32, 32), 32)
            value = gate[take, :]
            hidden[take, :] = (value / (1.0 + jnp.exp(-value)) * up[take, :]).astype(bf16)

        if r == 0:
            loads[2].wait()

    def down(r, p):
        bufs = buffers[r]
        shape = bufs["own"].shape[1:]
        other = pl.ds(pl.multiple_of(oh * half + p * piece, 128), piece)
        mine = pl.ds(pl.multiple_of(h * half + p * piece, 128), piece)
        bufs["a_send"][p] = jnp.dot(
            bufs["hidden"][...], dw[:, other], preferred_element_type=f32).astype(bf16).reshape(shape)
        sum_hid[r, p].start()
        bufs["own"][p] = jnp.dot(bufs["hidden"][...], dw[:, mine], preferred_element_type=f32).reshape(shape)

    def reduce_hid(r, p):
        bufs = buffers[r]
        sum_hid[r, p].wait_recv()
        bufs["b_send"][p] = (bufs["own"][p, ox] + bufs["a_recv"][p, ox].astype(f32)).astype(bf16)
        sum_blk[r, p].start()
        bufs["own"][p, x] = bufs["own"][p, x] + bufs["a_recv"][p, x].astype(f32)

    def reduce_blk(r, p):
        bufs = buffers[r]
        sum_blk[r, p].wait_recv()
        total = (bufs["own"][p, x] + bufs["b_recv"][p].astype(f32)).astype(bf16)
        bufs["c_send"][p] = total.reshape(bufs["c_send"].shape[1:])
        for copy in back[r, p]:
            copy.start()
        bufs["ret"][p, z] = bufs["c_send"][p, z]

    def combine(r, p):
        if r < len(rounds) - 1:
            return
        value = None
        for q in range(len(rounds)):
            for copy in back[q, p]:
                copy.wait_recv()
            result = buffers[q]["ret"][p].reshape(steps * rounds[q], piece)
            for mix in mixes[q]:
                term = jnp.dot(mix, result, preferred_element_type=f32)
                value = term if value is None else value + term
        out[:, p * piece:(p + 1) * piece] = value.astype(bf16)

    def staggered(r, stages):
        lines = []
        for i in range(pieces + len(stages) - 1):
            lines.append([(f, r, i - k) for k, f in enumerate(stages) if 0 <= i - k < pieces])
        return lines

    going = [staggered(r, (forward, forward2, compute)) for r in range(len(rounds))]
    coming = [staggered(r, (down, reduce_hid, reduce_blk, combine)) for r in range(len(rounds))]
    plan = [(build, 0, p) for p in range(pieces)]
    for load in loads:
        plan.append((lambda r, p, load=load: load.start(), 0, 0))
    plan += [(build, r, p) for r in range(1, len(rounds)) for p in range(pieces)]
    for r in range(len(rounds) + 1):
        go = going[r] if r < len(rounds) else []
        come = coming[r - 1] if r else []
        for i in range(max(len(go), len(come))):
            plan += (go[i] if i < len(go) else []) + (come[i] if i < len(come) else [])
        if r < len(rounds):
            plan.append((activate, r, 0))
    for function, r, p in plan:
        function(r, p)

    for key in work:
        for copy in to_expert[key] + back[key]:
            copy.wait_send()
        for group in (across, beside, beside2, sum_hid, sum_blk):
            group[key].wait_send()


def local_kernel(tokens, routes, scores, gate_weight, up_weight, down_weight):
    tok_dev, width = tokens.shape
    steps = lax.axis_size("outer")
    half = width // 2
    units = gate_weight.shape[1]
    capacity = (tok_dev * routes.shape[1] * 5 // steps + 3) // 4
    blocks = (capacity + 15) // 16
    rounds, left = [], blocks
    for part in range(len(ROUND_PARTS)):
        take = left if part == len(ROUND_PARTS) - 1 else blocks * ROUND_PARTS[part] // sum(ROUND_PARTS)
        rounds.append(16 * take)
        left -= take
    pieces = PIECES
    piece = half // pieces
    vmem, hbm = pl.BlockSpec(memory_space=pltpu.VMEM), pl.BlockSpec(memory_space=pl.ANY)
    buffers = []
    for c in rounds:
        buffers.append({
            "send": pltpu.VMEM((pieces, steps, c, piece), bf16),
            "rows": pltpu.VMEM((pieces, 2, 2, steps, c, piece), bf16),
            "gate": pltpu.VMEM((2 * steps * c, units), f32),
            "up": pltpu.VMEM((2 * steps * c, units), f32),
            "hidden": pltpu.VMEM((2 * steps * c, units), bf16),
            "own": pltpu.VMEM((pieces, 2, steps * c, piece), f32),
            "a_send": pltpu.VMEM((pieces, 2, steps * c, piece), bf16),
            "a_recv": pltpu.VMEM((pieces, 2, steps * c, piece), bf16),
            "b_send": pltpu.VMEM((pieces, steps * c, piece), bf16),
            "b_recv": pltpu.VMEM((pieces, steps * c, piece), bf16),
            "c_send": pltpu.VMEM((pieces, steps, c, piece), bf16),
            "ret": pltpu.VMEM((pieces, steps, c, piece), bf16),
        })
    number = len(rounds) * pieces
    dma = pltpu.SemaphoreType.DMA
    scratch = [
        pltpu.VMEM((tok_dev, half), bf16),
        pltpu.VMEM((units, width), bf16),
        pltpu.VMEM((units, width), bf16),
        pltpu.VMEM((units, width), bf16),
        buffers,
        dma((4,)),
        dma((number, steps)),
        dma((number, steps)),
        dma((5, number)),
        dma((5, number)),
        dma((number, steps)),
        dma((number, steps)),
    ]
    macs = 6 * steps * sum(rounds) * units * width
    return pl.pallas_call(
        functools.partial(layer_kernel, tuple(rounds), pieces),
        out_shape=jax.ShapeDtypeStruct((tok_dev, half), bf16),
        in_specs=[hbm, vmem, vmem, hbm, hbm, hbm],
        out_specs=vmem,
        scratch_shapes=scratch,
        compiler_params=pltpu.CompilerParams(
            collective_id=0, has_side_effects=True, vmem_limit_bytes=56 * 1024 * 1024),
        cost_estimate=pl.CostEstimate(flops=2 * macs, bytes_accessed=6 * units * width, transcendentals=0),
    )(tokens, routes, scores, gate_weight, up_weight, down_weight)


def solution(mesh):
    in_specs = (
        P(("group", "outer", "blk"), None),
        P(("group", "outer", "blk"), None),
        P(("group", "outer", "blk"), None),
        P("outer", ("blk", "hid"), None),
        P("outer", ("blk", "hid"), None),
        P("outer", ("blk", "hid"), None),
    )
    out_specs = P(("group", "outer", "blk"), "hid")
    fits = mesh.shape["outer"] == 4 and mesh.shape["blk"] == 2 and mesh.shape["hid"] == 2
    body = local_kernel if fits else local
    return jax.shard_map(body, mesh=mesh, in_specs=in_specs, out_specs=out_specs, check_vma=False)
```

```python
import functools
import jax
import jax.numpy as jnp
from jax import lax
from jax.experimental import pallas as pl
from jax.experimental.pallas import tpu as pltpu
from jax.sharding import PartitionSpec as P

route_scale = 2.5
PIECES = 7
WINDOW = 2
ROUND_PARTS = (1,)
SEND_ORDER = (2, 3, 1)


def slice_terms(rows, gate_piece, up_piece, down_piece):
    dims = (((1,), (1,)), ((), ()))
    gate_part = lax.dot_general(rows, gate_piece, dims, preferred_element_type=jnp.float32)
    up_part = lax.dot_general(rows, up_piece, dims, preferred_element_type=jnp.float32)
    hidden = (jax.nn.silu(gate_part) * up_part).astype(jnp.bfloat16)
    return jnp.dot(hidden, down_piece, preferred_element_type=jnp.float32)


def local(tokens, routes, scores, gate_weight, up_weight, down_weight):
    tok_dev, width = tokens.shape
    topk = routes.shape[1]
    experts = lax.axis_size("outer")
    shares = lax.axis_size("hid")
    half = width // shares
    capacity = (tok_dev * topk * 5 // experts + 3) // 4
    flat = routes.reshape(-1)
    onehot = (flat[:, None] == jnp.arange(experts, dtype=jnp.int32)[None, :]).astype(jnp.int32)
    before = jnp.cumsum(onehot, axis=0) - onehot
    rank = jnp.sum(before * onehot, axis=1)
    slots = flat * capacity + rank
    owner = jnp.arange(tok_dev * topk, dtype=jnp.int32) // topk
    columns = tokens.shape[1]
    send = jnp.zeros((experts * capacity, columns), jnp.bfloat16).at[slots].set(tokens[owner])
    send = send.reshape(experts, capacity, columns)
    gate_local = gate_weight[0]
    up_local = up_weight[0]
    down_local = down_weight[0]
    arrived = lax.all_to_all(send, "outer", split_axis=0, concat_axis=0, tiled=True)
    senders, count, unused = arrived.shape
    rows = arrived.reshape(senders * count, width)
    total = slice_terms(
        rows,
        lax.all_gather(gate_local, "blk", axis=0, tiled=True),
        lax.all_gather(up_local, "blk", axis=0, tiled=True),
        lax.all_gather(down_local, "blk", axis=0, tiled=True),
    )
    summed = lax.psum(total.astype(jnp.bfloat16), "hid").astype(jnp.float32)
    share = lax.dynamic_slice_in_dim(summed, lax.axis_index("hid") * half, half, 1)
    answered = share.astype(jnp.bfloat16).reshape(senders, count, half)
    returned = lax.all_to_all(answered, "outer", split_axis=0, concat_axis=0, tiled=True)
    picked = (
        returned.reshape(experts * capacity, half)[slots]
        .astype(jnp.float32)
        .reshape(tok_dev, topk, half)
    )
    weights = route_scale * scores / jnp.sum(scores, axis=1, keepdims=True)
    mixed = jnp.sum(weights[:, :, None] * picked, axis=1)
    return mixed.astype(jnp.bfloat16)


MESH = pl.DeviceIdType.MESH
bf16, f32 = jnp.bfloat16, jnp.float32


def partner(z, d):
    if d == 1:
        return z + 1 - 2 * lax.rem(z, 2)
    if d == 2:
        return lax.rem(z + 2, 4)
    if d == 3:
        return 3 - z
    return z


def layer_kernel(rounds, pieces, tok, routes, scores, gate_hbm, up_hbm, down_hbm, out,
                 tokv, gw, uw, dw, buffers, local_sem, z_s, z_r, sem_s, sem_r, back_s, back_r):
    z, x, h = lax.axis_index("outer"), lax.axis_index("blk"), lax.axis_index("hid")
    steps = buffers[0]["send"].shape[1]
    half, units = tokv.shape[1], gw.shape[0]
    piece = half // pieces
    ox, oh = 1 - x, 1 - h
    col0 = pl.multiple_of(h * half, 128)

    load_tok = pltpu.make_async_copy(tok.at[:, pl.ds(col0, half)], tokv, local_sem.at[0])
    load_tok.start()
    loads = [
        pltpu.make_async_copy(src.at[0], dst, local_sem.at[1 + i])
        for i, (src, dst) in enumerate(((gate_hbm, gw), (up_hbm, uw), (down_hbm, dw)))
    ]

    barrier = pltpu.get_barrier_semaphore()
    peers = [{"outer": partner(z, d)} for d in range(1, steps)] + [{"blk": ox}, {"hid": oh}]
    for peer in peers:
        pl.semaphore_signal(barrier, inc=1, device_id=peer, device_id_type=MESH)

    tokens = routes.shape[1]
    above = lax.broadcasted_iota(jnp.int32, (tokens, tokens), 0) < lax.broadcasted_iota(
        jnp.int32, (tokens, tokens), 1)
    above = jnp.where(above, 1.0, 0.0).astype(bf16)
    weight = route_scale * scores[...] / (scores[0:1, :] + scores[1:2, :])
    places, mixes = [], []
    start = 0
    for c in rounds:
        line = lax.broadcasted_iota(jnp.int32, (steps * c, tokens), 0)
        expert = line // c
        first = routes[0:1, :] == expert
        second = routes[1:2, :] == expert
        named = jnp.where(first | second, 1.0, 0.0)
        rank = jnp.dot(named.astype(bf16), above, preferred_element_type=f32)
        slot = (line - expert * c + start).astype(f32)
        place = jnp.where(rank == slot, named, 0.0)
        mix = place * (jnp.where(first, weight[0:1, :], 0.0) + jnp.where(second, weight[1:2, :], 0.0))
        mix_high = mix.astype(bf16)
        places.append(place.astype(bf16))
        mixes.append((mix_high, (mix - mix_high.astype(f32)).astype(bf16)))
        start += c

    where = [partner(z, d) for d in range(steps)]

    def remote(src, dst, send_sem, recv_sem, peer):
        return pltpu.make_async_remote_copy(
            src_ref=src, dst_ref=dst, send_sem=send_sem, recv_sem=recv_sem,
            device_id=peer, device_id_type=MESH)

    work = [(r, p) for r in range(len(rounds)) for p in range(pieces)]
    to_expert, across, beside, beside2, sum_hid, sum_blk, back = {}, {}, {}, {}, {}, {}, {}
    across_own, sum_blk_own = {}, {}
    for n, (r, p) in enumerate(work):
        bufs, key = buffers[r], (r, p)
        rows = bufs["rows"]
        to_expert[key] = [
            remote(bufs["send"].at[p, where[d]], rows.at[p, h, x, d], z_s.at[n, d], z_r.at[n, d], {"outer": where[d]})
            for d in SEND_ORDER]
        far = pl.ds(1, steps - 1)
        across[key] = remote(
            rows.at[p, h, x, far], rows.at[p, h, x, far], sem_s.at[0, n], sem_r.at[0, n], {"blk": ox})
        across_own[key] = remote(
            rows.at[p, h, x, 0], rows.at[p, h, x, 0], sem_s.at[5, n], sem_r.at[5, n], {"blk": ox})
        beside[key] = remote(rows.at[p, h, x], rows.at[p, h, x], sem_s.at[1, n], sem_r.at[1, n], {"hid": oh})
        beside2[key] = remote(rows.at[p, h, ox], rows.at[p, h, ox], sem_s.at[2, n], sem_r.at[2, n], {"hid": oh})
        sum_hid[key] = remote(bufs["a_send"].at[p], bufs["a_recv"].at[p], sem_s.at[3, n], sem_r.at[3, n], {"hid": oh})
        sum_blk[key] = remote(
            bufs["b_send"].at[p, far], bufs["b_recv"].at[p, far], sem_s.at[4, n], sem_r.at[4, n], {"blk": ox})
        sum_blk_own[key] = remote(
            bufs["b_send"].at[p, 0], bufs["b_recv"].at[p, 0], sem_s.at[6, n], sem_r.at[6, n], {"blk": ox})
        back[key] = [
            remote(bufs["c_send"].at[p, d], bufs["ret"].at[p, z], back_s.at[n, d], back_r.at[n, d], {"outer": where[d]})
            for d in SEND_ORDER]

    load_tok.wait()

    def build(r, p):
        sent = jnp.dot(places[r], tokv[:, p * piece:(p + 1) * piece], preferred_element_type=f32)
        buffers[r]["send"][p] = sent.astype(bf16).reshape(steps, rounds[r], piece)
        if (r, p) == work[0]:
            pl.semaphore_wait(barrier, len(peers))
        if work.index((r, p)) < WINDOW:
            for copy in to_expert[r, p]:
                copy.start()
        buffers[r]["rows"][p, h, x, 0] = buffers[r]["send"][p, z]
        across_own[r, p].start()

    def forward(r, p):
        n = work.index((r, p)) + WINDOW
        if n < len(work):
            for copy in to_expert[work[n]]:
                copy.start()
        for copy in to_expert[r, p]:
            copy.wait_recv()
        across[r, p].start()
        beside[r, p].start()

    def forward2(r, p):
        across_own[r, p].wait_recv()
        across[r, p].wait_recv()
        beside2[r, p].start()

    nt = (((1,), (1,)), ((), ()))

    def compute(r, p):
        bufs = buffers[r]
        rows, gate, up = bufs["rows"], bufs["gate"], bufs["up"]
        beside[r, p].wait_recv()
        beside2[r, p].wait_recv()
        if (r, p) == work[0]:
            loads[0].wait()
            loads[1].wait()
        parts = [rows[p, k].reshape(gate.shape[0], piece) for k in range(2)]

        @pl.loop(0, units // 256)
        def _(j):
            take = pl.ds(pl.multiple_of(j * 256, 256), 256)
            for total, weights in ((gate, gw), (up, uw)):
                value = sum(
                    lax.dot_general(
                        parts[k], weights[take, k * half + p * piece:k * half + (p + 1) * piece], nt,
                        preferred_element_type=f32)
                    for k in range(2))
                total[:, take] = value if p == 0 else total[:, take] + value

    def activate(r, p):
        bufs = buffers[r]
        gate, up, hidden = bufs["gate"], bufs["up"], bufs["hidden"]

        @pl.loop(0, gate.shape[0] // 32)
        def _(j):
            take = pl.ds(pl.multiple_of(j * 32, 32), 32)
            value = gate[take, :]
            hidden[take, :] = (value / (1.0 + jnp.exp(-value)) * up[take, :]).astype(bf16)

        if r == 0:
            loads[2].wait()

    def down(r, p):
        bufs = buffers[r]
        shape = bufs["own"].shape[1:]
        other = pl.ds(pl.multiple_of(oh * half + p * piece, 128), piece)
        mine = pl.ds(pl.multiple_of(h * half + p * piece, 128), piece)
        bufs["a_send"][p] = jnp.dot(
            bufs["hidden"][...], dw[:, other], preferred_element_type=f32).astype(bf16).reshape(shape)
        sum_hid[r, p].start()
        bufs["own"][p] = jnp.dot(bufs["hidden"][...], dw[:, mine], preferred_element_type=f32).reshape(shape)

    def reduce_hid(r, p):
        bufs = buffers[r]
        sum_hid[r, p].wait_recv()
        bufs["b_send"][p] = (bufs["own"][p, ox] + bufs["a_recv"][p, ox].astype(f32)).astype(bf16)
        sum_blk[r, p].start()
        if p == pieces - 1:
            for q in range(pieces):
                sum_blk_own[r, q].start()
        bufs["own"][p, x] = bufs["own"][p, x] + bufs["a_recv"][p, x].astype(f32)

    def reduce_blk(r, p):
        bufs = buffers[r]
        sum_blk[r, p].wait_recv()
        bufs["c_send"][p, 1:] = (bufs["own"][p, x, 1:] + bufs["b_recv"][p, 1:].astype(f32)).astype(bf16)
        for copy in back[r, p]:
            copy.start()

    def reduce_own(r, p):
        bufs = buffers[r]
        sum_blk_own[r, p].wait_recv()
        bufs["ret"][p, z] = (bufs["own"][p, x, 0] + bufs["b_recv"][p, 0].astype(f32)).astype(bf16)

    def combine(r, p):
        if r < len(rounds) - 1:
            return
        value = None
        for q in range(len(rounds)):
            for copy in back[q, p]:
                copy.wait_recv()
            result = buffers[q]["ret"][p].reshape(steps * rounds[q], piece)
            for mix in mixes[q]:
                term = lax.dot_general(mix, result, (((0,), (0,)), ((), ())), preferred_element_type=f32)
                value = term if value is None else value + term
        out[:, p * piece:(p + 1) * piece] = value.astype(bf16)

    def staggered(r, stages):
        lines = []
        for i in range(pieces + len(stages) - 1):
            lines.append([(f, r, i - k) for k, f in enumerate(stages) if 0 <= i - k < pieces])
        return lines

    going = [staggered(r, (forward, forward2, compute)) for r in range(len(rounds))]
    coming = [
        staggered(r, (down, reduce_hid, reduce_blk))
        + [[(reduce_own, r, p), (combine, r, p)] for p in range(pieces)]
        for r in range(len(rounds))
    ]
    plan = [(build, 0, p) for p in range(pieces)]
    for load in loads:
        plan.append((lambda r, p, load=load: load.start(), 0, 0))
    plan += [(build, r, p) for r in range(1, len(rounds)) for p in range(pieces)]
    for r in range(len(rounds) + 1):
        go = going[r] if r < len(rounds) else []
        come = coming[r - 1] if r else []
        for i in range(max(len(go), len(come))):
            plan += (go[i] if i < len(go) else []) + (come[i] if i < len(come) else [])
        if r < len(rounds):
            plan.append((activate, r, 0))
    for function, r, p in plan:
        function(r, p)

    for key in work:
        for copy in to_expert[key] + back[key]:
            copy.wait_send()
        for group in (across, across_own, beside, beside2, sum_hid, sum_blk, sum_blk_own):
            group[key].wait_send()


def local_kernel(tokens, routes, scores, gate_weight, up_weight, down_weight):
    tok_dev, width = tokens.shape
    steps = lax.axis_size("outer")
    half = width // 2
    units = gate_weight.shape[1]
    capacity = (tok_dev * routes.shape[1] * 5 // steps + 3) // 4
    blocks = (capacity + 15) // 16
    rounds, left = [], blocks
    for part in range(len(ROUND_PARTS)):
        take = left if part == len(ROUND_PARTS) - 1 else blocks * ROUND_PARTS[part] // sum(ROUND_PARTS)
        rounds.append(16 * take)
        left -= take
    pieces = PIECES
    piece = half // pieces
    vmem, hbm = pl.BlockSpec(memory_space=pltpu.VMEM), pl.BlockSpec(memory_space=pl.ANY)
    buffers = []
    for c in rounds:
        buffers.append({
            "send": pltpu.VMEM((pieces, steps, c, piece), bf16),
            "rows": pltpu.VMEM((pieces, 2, 2, steps, c, piece), bf16),
            "gate": pltpu.VMEM((2 * steps * c, units), f32),
            "up": pltpu.VMEM((2 * steps * c, units), f32),
            "hidden": pltpu.VMEM((2 * steps * c, units), bf16),
            "own": pltpu.VMEM((pieces, 2, steps, c, piece), f32),
            "a_send": pltpu.VMEM((pieces, 2, steps, c, piece), bf16),
            "a_recv": pltpu.VMEM((pieces, 2, steps, c, piece), bf16),
            "b_send": pltpu.VMEM((pieces, steps, c, piece), bf16),
            "b_recv": pltpu.VMEM((pieces, steps, c, piece), bf16),
            "c_send": pltpu.VMEM((pieces, steps, c, piece), bf16),
            "ret": pltpu.VMEM((pieces, steps, c, piece), bf16),
        })
    number = len(rounds) * pieces
    dma = pltpu.SemaphoreType.DMA
    scratch = [
        pltpu.VMEM((tok_dev, half), bf16),
        pltpu.VMEM((units, width), bf16),
        pltpu.VMEM((units, width), bf16),
        pltpu.VMEM((units, width), bf16),
        buffers,
        dma((4,)),
        dma((number, steps)),
        dma((number, steps)),
        dma((7, number)),
        dma((7, number)),
        dma((number, steps)),
        dma((number, steps)),
    ]
    macs = 6 * steps * sum(rounds) * units * width
    return pl.pallas_call(
        functools.partial(layer_kernel, tuple(rounds), pieces),
        out_shape=jax.ShapeDtypeStruct((tok_dev, half), bf16),
        in_specs=[hbm, vmem, vmem, hbm, hbm, hbm],
        out_specs=vmem,
        scratch_shapes=scratch,
        compiler_params=pltpu.CompilerParams(
            collective_id=0, has_side_effects=True, vmem_limit_bytes=56 * 1024 * 1024),
        cost_estimate=pl.CostEstimate(flops=2 * macs, bytes_accessed=6 * units * width, transcendentals=0),
    )(tokens, routes.T, scores.T, gate_weight, up_weight, down_weight)


def solution(mesh):
    in_specs = (
        P(("group", "outer", "blk"), None),
        P(("group", "outer", "blk"), None),
        P(("group", "outer", "blk"), None),
        P("outer", ("blk", "hid"), None),
        P("outer", ("blk", "hid"), None),
        P("outer", ("blk", "hid"), None),
    )
    out_specs = P(("group", "outer", "blk"), "hid")
    fits = mesh.shape["outer"] == 4 and mesh.shape["blk"] == 2 and mesh.shape["hid"] == 2
    body = local_kernel if fits else local
    return jax.shard_map(body, mesh=mesh, in_specs=in_specs, out_specs=out_specs, check_vma=False)
```

```python
import functools
import jax
import jax.numpy as jnp
from jax import lax
from jax.experimental import pallas as pl
from jax.experimental.pallas import tpu as pltpu
from jax.sharding import PartitionSpec as P

route_scale = 2.5
PIECES = 7
WINDOW = 2
ROUND_PARTS = (1,)
SEND_ORDER = (3, 2, 1)


def slice_terms(rows, gate_piece, up_piece, down_piece):
    dims = (((1,), (1,)), ((), ()))
    gate_part = lax.dot_general(rows, gate_piece, dims, preferred_element_type=jnp.float32)
    up_part = lax.dot_general(rows, up_piece, dims, preferred_element_type=jnp.float32)
    hidden = (jax.nn.silu(gate_part) * up_part).astype(jnp.bfloat16)
    return jnp.dot(hidden, down_piece, preferred_element_type=jnp.float32)


def local(tokens, routes, scores, gate_weight, up_weight, down_weight):
    tok_dev, width = tokens.shape
    topk = routes.shape[1]
    experts = lax.axis_size("outer")
    shares = lax.axis_size("hid")
    half = width // shares
    capacity = (tok_dev * topk * 5 // experts + 3) // 4
    flat = routes.reshape(-1)
    onehot = (flat[:, None] == jnp.arange(experts, dtype=jnp.int32)[None, :]).astype(jnp.int32)
    before = jnp.cumsum(onehot, axis=0) - onehot
    rank = jnp.sum(before * onehot, axis=1)
    slots = flat * capacity + rank
    owner = jnp.arange(tok_dev * topk, dtype=jnp.int32) // topk
    columns = tokens.shape[1]
    send = jnp.zeros((experts * capacity, columns), jnp.bfloat16).at[slots].set(tokens[owner])
    send = send.reshape(experts, capacity, columns)
    gate_local = gate_weight[0]
    up_local = up_weight[0]
    down_local = down_weight[0]
    arrived = lax.all_to_all(send, "outer", split_axis=0, concat_axis=0, tiled=True)
    senders, count, unused = arrived.shape
    rows = arrived.reshape(senders * count, width)
    total = slice_terms(
        rows,
        lax.all_gather(gate_local, "blk", axis=0, tiled=True),
        lax.all_gather(up_local, "blk", axis=0, tiled=True),
        lax.all_gather(down_local, "blk", axis=0, tiled=True),
    )
    summed = lax.psum(total.astype(jnp.bfloat16), "hid").astype(jnp.float32)
    share = lax.dynamic_slice_in_dim(summed, lax.axis_index("hid") * half, half, 1)
    answered = share.astype(jnp.bfloat16).reshape(senders, count, half)
    returned = lax.all_to_all(answered, "outer", split_axis=0, concat_axis=0, tiled=True)
    picked = (
        returned.reshape(experts * capacity, half)[slots]
        .astype(jnp.float32)
        .reshape(tok_dev, topk, half)
    )
    weights = route_scale * scores / jnp.sum(scores, axis=1, keepdims=True)
    mixed = jnp.sum(weights[:, :, None] * picked, axis=1)
    return mixed.astype(jnp.bfloat16)


MESH = pl.DeviceIdType.MESH
bf16, f32 = jnp.bfloat16, jnp.float32


def partner(z, d):
    if d == 1:
        return z + 1 - 2 * lax.rem(z, 2)
    if d == 2:
        return lax.rem(z + 2, 4)
    if d == 3:
        return 3 - z
    return z


def layer_kernel(rounds, pieces, tok, routes, scores, gate_hbm, up_hbm, down_hbm, out,
                 tokv, gw, uw, dw, buffers, local_sem, z_s, z_r, sem_s, sem_r, back_s, back_r):
    z, x, h = lax.axis_index("outer"), lax.axis_index("blk"), lax.axis_index("hid")
    steps = buffers[0]["send"].shape[1]
    half, units = tokv.shape[1], gw.shape[0]
    piece = half // pieces
    ox, oh = 1 - x, 1 - h
    col0 = pl.multiple_of(h * half, 128)

    load_tok = pltpu.make_async_copy(tok.at[:, pl.ds(col0, half)], tokv, local_sem.at[0])
    load_tok.start()
    loads = [
        pltpu.make_async_copy(src.at[0], dst, local_sem.at[1 + i])
        for i, (src, dst) in enumerate(((gate_hbm, gw), (up_hbm, uw), (down_hbm, dw)))
    ]

    barrier = pltpu.get_barrier_semaphore()
    peers = [{"outer": partner(z, d)} for d in range(1, steps)] + [{"blk": ox}, {"hid": oh}]
    for peer in peers:
        pl.semaphore_signal(barrier, inc=1, device_id=peer, device_id_type=MESH)

    tokens = routes.shape[1]
    above = lax.broadcasted_iota(jnp.int32, (tokens, tokens), 0) < lax.broadcasted_iota(
        jnp.int32, (tokens, tokens), 1)
    above = jnp.where(above, 1.0, 0.0).astype(bf16)
    weight = route_scale * scores[...] / (scores[0:1, :] + scores[1:2, :])
    places, mixes = [], []
    start = 0
    for c in rounds:
        line = lax.broadcasted_iota(jnp.int32, (steps * c, tokens), 0)
        expert = line // c
        first = routes[0:1, :] == expert
        second = routes[1:2, :] == expert
        named = jnp.where(first | second, 1.0, 0.0)
        rank = jnp.dot(named.astype(bf16), above, preferred_element_type=f32)
        slot = (line - expert * c + start).astype(f32)
        place = jnp.where(rank == slot, named, 0.0)
        mix = place * (jnp.where(first, weight[0:1, :], 0.0) + jnp.where(second, weight[1:2, :], 0.0))
        mix_high = mix.astype(bf16)
        places.append(place.astype(bf16))
        mixes.append((mix_high, (mix - mix_high.astype(f32)).astype(bf16)))
        start += c

    where = [partner(z, d) for d in range(steps)]

    def remote(src, dst, send_sem, recv_sem, peer):
        return pltpu.make_async_remote_copy(
            src_ref=src, dst_ref=dst, send_sem=send_sem, recv_sem=recv_sem,
            device_id=peer, device_id_type=MESH)

    work = [(r, p) for r in range(len(rounds)) for p in range(pieces)]
    to_expert, across, beside, beside2, sum_hid, sum_blk, back = {}, {}, {}, {}, {}, {}, {}
    across_own, sum_blk_own = {}, {}
    for n, (r, p) in enumerate(work):
        bufs, key = buffers[r], (r, p)
        rows = bufs["rows"]
        to_expert[key] = [
            remote(bufs["send"].at[p, where[d]], rows.at[p, h, x, d], z_s.at[n, d], z_r.at[n, d], {"outer": where[d]})
            for d in SEND_ORDER]
        far = pl.ds(1, steps - 1)
        across[key] = remote(
            rows.at[p, h, x, far], rows.at[p, h, x, far], sem_s.at[0, n], sem_r.at[0, n], {"blk": ox})
        across_own[key] = remote(
            rows.at[p, h, x, 0], rows.at[p, h, x, 0], sem_s.at[5, n], sem_r.at[5, n], {"blk": ox})
        beside[key] = remote(rows.at[p, h, x], rows.at[p, h, x], sem_s.at[1, n], sem_r.at[1, n], {"hid": oh})
        beside2[key] = remote(rows.at[p, h, ox], rows.at[p, h, ox], sem_s.at[2, n], sem_r.at[2, n], {"hid": oh})
        sum_hid[key] = remote(bufs["a_send"].at[p], bufs["a_recv"].at[p], sem_s.at[3, n], sem_r.at[3, n], {"hid": oh})
        sum_blk[key] = remote(
            bufs["b_send"].at[p, far], bufs["b_recv"].at[p, far], sem_s.at[4, n], sem_r.at[4, n], {"blk": ox})
        sum_blk_own[key] = remote(
            bufs["b_send"].at[p, 0], bufs["b_recv"].at[p, 0], sem_s.at[6, n], sem_r.at[6, n], {"blk": ox})
        back[key] = [
            remote(bufs["c_send"].at[p, d], bufs["ret"].at[p, z], back_s.at[n, d], back_r.at[n, d], {"outer": where[d]})
            for d in SEND_ORDER]

    load_tok.wait()

    def build(r, p):
        sent = jnp.dot(places[r], tokv[:, p * piece:(p + 1) * piece], preferred_element_type=f32)
        buffers[r]["send"][p] = sent.astype(bf16).reshape(steps, rounds[r], piece)
        if (r, p) == work[0]:
            pl.semaphore_wait(barrier, len(peers))
        if work.index((r, p)) < WINDOW:
            for copy in to_expert[r, p]:
                copy.start()
        buffers[r]["rows"][p, h, x, 0] = buffers[r]["send"][p, z]
        across_own[r, p].start()

    def forward(r, p):
        n = work.index((r, p)) + WINDOW
        if n < len(work):
            for copy in to_expert[work[n]]:
                copy.start()
        for copy in to_expert[r, p]:
            copy.wait_recv()
        across[r, p].start()
        beside[r, p].start()

    def forward2(r, p):
        across_own[r, p].wait_recv()
        across[r, p].wait_recv()
        beside2[r, p].start()

    nt = (((1,), (1,)), ((), ()))

    def compute(r, p):
        bufs = buffers[r]
        rows, gate, up = bufs["rows"], bufs["gate"], bufs["up"]
        beside[r, p].wait_recv()
        beside2[r, p].wait_recv()
        if (r, p) == work[0]:
            loads[0].wait()
            loads[1].wait()
        parts = [rows[p, k].reshape(gate.shape[0], piece) for k in range(2)]

        @pl.loop(0, units // 256)
        def _(j):
            take = pl.ds(pl.multiple_of(j * 256, 256), 256)
            for total, weights in ((gate, gw), (up, uw)):
                value = sum(
                    lax.dot_general(
                        parts[k], weights[take, k * half + p * piece:k * half + (p + 1) * piece], nt,
                        preferred_element_type=f32)
                    for k in range(2))
                total[:, take] = value if p == 0 else total[:, take] + value

    def activate(r, p):
        bufs = buffers[r]
        gate, up, hidden = bufs["gate"], bufs["up"], bufs["hidden"]

        @pl.loop(0, gate.shape[0] // 32)
        def _(j):
            take = pl.ds(pl.multiple_of(j * 32, 32), 32)
            value = gate[take, :]
            hidden[take, :] = (value / (1.0 + jnp.exp(-value)) * up[take, :]).astype(bf16)

        if r == 0:
            loads[2].wait()

    def down(r, p):
        bufs = buffers[r]
        shape = bufs["own"].shape[1:]
        other = pl.ds(pl.multiple_of(oh * half + p * piece, 128), piece)
        mine = pl.ds(pl.multiple_of(h * half + p * piece, 128), piece)
        bufs["a_send"][p] = jnp.dot(
            bufs["hidden"][...], dw[:, other], preferred_element_type=f32).astype(bf16).reshape(shape)
        sum_hid[r, p].start()
        bufs["own"][p] = jnp.dot(bufs["hidden"][...], dw[:, mine], preferred_element_type=f32).reshape(shape)

    def reduce_hid(r, p):
        bufs = buffers[r]
        sum_hid[r, p].wait_recv()
        bufs["b_send"][p] = (bufs["own"][p, ox] + bufs["a_recv"][p, ox].astype(f32)).astype(bf16)
        sum_blk[r, p].start()
        if p == pieces - 1:
            for q in range(pieces):
                sum_blk_own[r, q].start()
        bufs["own"][p, x] = bufs["own"][p, x] + bufs["a_recv"][p, x].astype(f32)

    def reduce_blk(r, p):
        bufs = buffers[r]
        sum_blk[r, p].wait_recv()
        bufs["c_send"][p, 1:] = (bufs["own"][p, x, 1:] + bufs["b_recv"][p, 1:].astype(f32)).astype(bf16)
        for copy in back[r, p]:
            copy.start()

    def reduce_own(r, p):
        bufs = buffers[r]
        sum_blk_own[r, p].wait_recv()
        bufs["ret"][p, z] = (bufs["own"][p, x, 0] + bufs["b_recv"][p, 0].astype(f32)).astype(bf16)

    def combine(r, p):
        if r < len(rounds) - 1:
            return
        value = None
        for q in range(len(rounds)):
            for copy in back[q, p]:
                copy.wait_recv()
            result = buffers[q]["ret"][p].reshape(steps * rounds[q], piece)
            for mix in mixes[q]:
                term = lax.dot_general(mix, result, (((0,), (0,)), ((), ())), preferred_element_type=f32)
                value = term if value is None else value + term
        out[:, p * piece:(p + 1) * piece] = value.astype(bf16)

    def staggered(r, stages):
        lines = []
        for i in range(pieces + len(stages) - 1):
            lines.append([(f, r, i - k) for k, f in enumerate(stages) if 0 <= i - k < pieces])
        return lines

    going = [staggered(r, (forward, forward2, compute)) for r in range(len(rounds))]
    coming = [
        staggered(r, (down, reduce_hid, reduce_blk))
        + [[(reduce_own, r, p), (combine, r, p)] for p in range(pieces)]
        for r in range(len(rounds))
    ]
    plan = [(build, 0, p) for p in range(pieces)]
    for load in loads:
        plan.append((lambda r, p, load=load: load.start(), 0, 0))
    plan += [(build, r, p) for r in range(1, len(rounds)) for p in range(pieces)]
    for r in range(len(rounds) + 1):
        go = going[r] if r < len(rounds) else []
        come = coming[r - 1] if r else []
        for i in range(max(len(go), len(come))):
            plan += (go[i] if i < len(go) else []) + (come[i] if i < len(come) else [])
        if r < len(rounds):
            plan.append((activate, r, 0))
    for function, r, p in plan:
        function(r, p)

    for key in work:
        for copy in to_expert[key] + back[key]:
            copy.wait_send()
        for group in (across, across_own, beside, beside2, sum_hid, sum_blk, sum_blk_own):
            group[key].wait_send()


def local_kernel(tokens, routes, scores, gate_weight, up_weight, down_weight):
    tok_dev, width = tokens.shape
    steps = lax.axis_size("outer")
    half = width // 2
    units = gate_weight.shape[1]
    capacity = (tok_dev * routes.shape[1] * 5 // steps + 3) // 4
    blocks = (capacity + 15) // 16
    rounds, left = [], blocks
    for part in range(len(ROUND_PARTS)):
        take = left if part == len(ROUND_PARTS) - 1 else blocks * ROUND_PARTS[part] // sum(ROUND_PARTS)
        rounds.append(16 * take)
        left -= take
    pieces = PIECES
    piece = half // pieces
    vmem, hbm = pl.BlockSpec(memory_space=pltpu.VMEM), pl.BlockSpec(memory_space=pl.ANY)
    buffers = []
    for c in rounds:
        buffers.append({
            "send": pltpu.VMEM((pieces, steps, c, piece), bf16),
            "rows": pltpu.VMEM((pieces, 2, 2, steps, c, piece), bf16),
            "gate": pltpu.VMEM((2 * steps * c, units), f32),
            "up": pltpu.VMEM((2 * steps * c, units), f32),
            "hidden": pltpu.VMEM((2 * steps * c, units), bf16),
            "own": pltpu.VMEM((pieces, 2, steps, c, piece), f32),
            "a_send": pltpu.VMEM((pieces, 2, steps, c, piece), bf16),
            "a_recv": pltpu.VMEM((pieces, 2, steps, c, piece), bf16),
            "b_send": pltpu.VMEM((pieces, steps, c, piece), bf16),
            "b_recv": pltpu.VMEM((pieces, steps, c, piece), bf16),
            "c_send": pltpu.VMEM((pieces, steps, c, piece), bf16),
            "ret": pltpu.VMEM((pieces, steps, c, piece), bf16),
        })
    number = len(rounds) * pieces
    dma = pltpu.SemaphoreType.DMA
    scratch = [
        pltpu.VMEM((tok_dev, half), bf16),
        pltpu.VMEM((units, width), bf16),
        pltpu.VMEM((units, width), bf16),
        pltpu.VMEM((units, width), bf16),
        buffers,
        dma((4,)),
        dma((number, steps)),
        dma((number, steps)),
        dma((7, number)),
        dma((7, number)),
        dma((number, steps)),
        dma((number, steps)),
    ]
    macs = 6 * steps * sum(rounds) * units * width
    return pl.pallas_call(
        functools.partial(layer_kernel, tuple(rounds), pieces),
        out_shape=jax.ShapeDtypeStruct((tok_dev, half), bf16),
        in_specs=[hbm, vmem, vmem, hbm, hbm, hbm],
        out_specs=vmem,
        scratch_shapes=scratch,
        compiler_params=pltpu.CompilerParams(
            collective_id=0, has_side_effects=True, vmem_limit_bytes=56 * 1024 * 1024),
        cost_estimate=pl.CostEstimate(flops=2 * macs, bytes_accessed=6 * units * width, transcendentals=0),
    )(tokens, routes.T, scores.T, gate_weight, up_weight, down_weight)


def solution(mesh):
    in_specs = (
        P(("group", "outer", "blk"), None),
        P(("group", "outer", "blk"), None),
        P(("group", "outer", "blk"), None),
        P("outer", ("blk", "hid"), None),
        P("outer", ("blk", "hid"), None),
        P("outer", ("blk", "hid"), None),
    )
    out_specs = P(("group", "outer", "blk"), "hid")
    fits = mesh.shape["outer"] == 4 and mesh.shape["blk"] == 2 and mesh.shape["hid"] == 2
    body = local_kernel if fits else local
    return jax.shard_map(body, mesh=mesh, in_specs=in_specs, out_specs=out_specs, check_vma=False)
```
